32 devices in a mesh: seq: 16 (over z, x, core), fsdp: 2 (over y).
Axes of the slice: x: 2, y: 2, z: 4, core: 2. Of those that a mesh axis runs over, the one named last changes fastest.
Arguments:
- text_states: bfloat16 [4096, 8192], P('seq'), may hold values from -6 to 6
- images: bfloat16 [16, 1601, 8192], P('seq', None, 'fsdp'), may hold values from -6 to 6
- norm_gain: float32 [8192], replicated, may hold values from 0.1 to 1.9
- query_weight: bfloat16 [8192, 4096], P('seq', 'fsdp'), may hold values from -0.0625 to 0.0625
- image_projection_weight: bfloat16 [8192, 2048], P(('fsdp', 'seq')), may hold values from -0.0625 to 0.0625
- query_gain: float32 [128], replicated, may hold values from 0.5 to 2
- key_gain: float32 [128], replicated, may hold values from 0.5 to 2
- admission: int32 [16, 16], P('seq'), may hold values from 0 to 1, as said below
Outputs:
- attended: bfloat16 [4096, 4096], P('seq', 'fsdp')
The draws below stay inside these ranges and needn't reach their ends.
Inputs may be any that keep to these rules, and one draw needn't show every extreme that they name: admission[c, m] is 1 for m = c and for at most 2 of the images m with c - 4 <= m < c, and 0 elsewhere; in every draw some text blocks, the last one among them, attend to exactly 3 images.
All inputs are finite; a program needn't handle non-finite values.
Results may differ from the reference program's by a relative error of at most 0.035.
Values may be sent and summed in bfloat16 or wider, within the bound.
A program may use at most 128 MiB of HBM per device.

```python
import math
import jax
import jax.numpy as jnp
from jax import lax

MODEL_WIDTH = 8192
QUERY_HEADS = 32
KEY_VALUE_HEADS = 8
HEAD_SIZE = 128
IMAGE_TOKENS = 1601
TEXT_TOKENS = 256
IMAGE_LOOKBACK = 4
MOST = 3
SPANS = 16
IMAGES = 16
TEXT = 4096
N_FSDP = 2


def gain_pair(key, stream_id):
    return jax.random.uniform(jax.random.fold_in(key, stream_id), (HEAD_SIZE,), jnp.float32, 0.5, 2.0)


def draw_query_gain(key, part):
    return gain_pair(key, 1)


def draw_key_gain(key, part):
    return gain_pair(key, 2)


def draw_admission(key, part):
    span_ids = jnp.arange(SPANS, dtype=jnp.int32)[:, None]
    image_ids = jnp.arange(IMAGES, dtype=jnp.int32)[None, :]
    distance = span_ids - image_ids
    candidate = (distance >= 1) & (distance <= IMAGE_LOOKBACK)
    priority = jax.random.randint(jax.random.fold_in(key, 1), (SPANS, IMAGES), 0, 1 << 20, dtype=jnp.int32) * IMAGES + image_ids
    outranked = jnp.sum((priority[:, None, :] > priority[:, :, None]) & candidate[:, None, :], axis=2)
    crowded = jax.random.randint(jax.random.fold_in(key, 2), (SPANS,), 0, 4, dtype=jnp.int32) == 0
    forced = jax.random.randint(jax.random.fold_in(key, 3), (), IMAGE_LOOKBACK, SPANS, dtype=jnp.int32)
    span_line = jnp.arange(SPANS, dtype=jnp.int32)
    crowded = crowded | (span_line == forced) | (span_line == SPANS - 1)
    extra_slots = jnp.where(crowded, MOST - 1, 0)[:, None]
    admitted = (distance == 0) | candidate & (outranked < extra_slots)
    return admitted.astype(jnp.int32)


def steps_of(rng, extent, split, least, high):
    factor_of = 1.0
    for position, blocks in split:
        draws = jax.random.uniform(jax.random.fold_in(jax.random.fold_in(rng, 6), position), (blocks,), jnp.float32, least / len(split), high / len(split))
        factor_of = factor_of * jnp.repeat(jnp.exp(draws), extent[position] // blocks).reshape((-1,) + (1,) * (len(extent) - 1 - position))
    return factor_of


def centred(own_key, shape, scale, limit, split=(), held_as=jnp.bfloat16):
    drawn = jax.random.normal(own_key, shape, jnp.float32) * scale
    if len(split) > 0:
        drawn = steps_of(own_key, shape, split, -0.22, 0.18) * drawn
    return jnp.clip(drawn, min=-limit, max=limit).astype(held_as)


def setup_inputs(seed: int = 0) -> dict:
    splits = jax.random.split(jax.random.key(seed), 9)
    return {
        "text_states": centred(splits[0], (TEXT, MODEL_WIDTH), 1.0, 6.0, ((0, 16),)),
        "images": centred(splits[1], (IMAGES, IMAGE_TOKENS, MODEL_WIDTH), 1.0, 6.0, ((0, 16), (2, 2))),
        "norm_gain": jnp.clip(1.0 + 0.18 * jax.random.normal(splits[2], (MODEL_WIDTH,), jnp.float32), 0.1, 1.9),
        "query_weight": centred(splits[3], (MODEL_WIDTH, QUERY_HEADS * HEAD_SIZE), MODEL_WIDTH ** -0.5, 0.0625, ((0, 16), (1, 2))),
        "image_projection_weight": centred(splits[4], (MODEL_WIDTH, KEY_VALUE_HEADS * 2 * HEAD_SIZE), MODEL_WIDTH ** -0.5, 0.0625, ((0, 32),)),
        "query_gain": draw_query_gain(jax.random.fold_in(splits[8], 71), 0),
        "key_gain": draw_key_gain(jax.random.fold_in(splits[8], 71), 0),
        "admission": draw_admission(jax.random.fold_in(splits[8], 71), 0),
    }


def rms_scale(values, gain):
    return values * lax.rsqrt(lax.optimization_barrier(jnp.mean(values * values, axis=-1, keepdims=True)) + 1e-05) * gain

def reference(text_states, images, norm_gain, query_weight, image_projection_weight, query_gain, key_gain, admission):
    normed = rms_scale(text_states.astype(jnp.float32), norm_gain).astype(jnp.bfloat16)
    queries = jnp.dot(normed, query_weight, preferred_element_type=jnp.float32).reshape(TEXT, QUERY_HEADS, HEAD_SIZE)
    query_heads = rms_scale(queries, query_gain).astype(jnp.bfloat16)
    block_width = MODEL_WIDTH // N_FSDP

    def project(image_rows):
        score_product = jnp.zeros((IMAGE_TOKENS, KEY_VALUE_HEADS * 2 * HEAD_SIZE), jnp.float32)
        for block in range(N_FSDP):
            partial_term = jnp.dot(image_rows[:, block * block_width:(block + 1) * block_width], image_projection_weight[block * block_width:(block + 1) * block_width], preferred_element_type=jnp.float32)
            rounded_term = lax.optimization_barrier(partial_term.astype(jnp.bfloat16))
            score_product = score_product + rounded_term.astype(jnp.float32)
        score_product = score_product.reshape(IMAGE_TOKENS, KEY_VALUE_HEADS, 2 * HEAD_SIZE)
        key_part = rms_scale(score_product[..., :HEAD_SIZE], key_gain)
        packed = jnp.concatenate([key_part, score_product[..., HEAD_SIZE:]], axis=-1).astype(jnp.bfloat16)
        return jnp.transpose(packed, (1, 0, 2))
    image_key_value = lax.map(project, images)
    padded_images = jnp.concatenate([jnp.zeros((IMAGE_LOOKBACK, KEY_VALUE_HEADS, IMAGE_TOKENS, 2 * HEAD_SIZE), jnp.bfloat16), image_key_value], axis=0)
    heads_per_group = QUERY_HEADS // KEY_VALUE_HEADS
    score_scale = 1.0 / math.sqrt(HEAD_SIZE)

    def span_out(operands):
        span_index, query_block_rows, admit_row = operands
        image_window = lax.dynamic_slice_in_dim(padded_images, span_index, IMAGE_LOOKBACK + 1, 0)
        image_ids = span_index - IMAGE_LOOKBACK + jnp.arange(IMAGE_LOOKBACK + 1, dtype=jnp.int32)
        admitted = (image_ids >= 0) & (jnp.take(admit_row, jnp.maximum(image_ids, 0).astype(jnp.int32)) == 1)
        column_live = jnp.repeat(admitted, IMAGE_TOKENS)
        key_value_pair = jnp.moveaxis(image_window, 1, 0).reshape(KEY_VALUE_HEADS, (IMAGE_LOOKBACK + 1) * IMAGE_TOKENS, 2 * HEAD_SIZE).astype(jnp.float32)
        query_widened = query_block_rows.reshape(TEXT_TOKENS, KEY_VALUE_HEADS, heads_per_group, HEAD_SIZE).astype(jnp.float32)
        scores = jnp.einsum('tkgd,knd->kgtn', query_widened, key_value_pair[..., :HEAD_SIZE]) * score_scale
        scores = jnp.where(column_live, scores, -jnp.inf)
        row_peak = lax.optimization_barrier(jnp.max(scores, axis=-1, keepdims=True))
        weights = jnp.exp(scores - row_peak)
        row_total = lax.optimization_barrier(jnp.sum(weights, axis=-1, keepdims=True))
        rounded = lax.optimization_barrier(weights.astype(jnp.bfloat16)).astype(jnp.float32)
        blended = jnp.einsum('kgtn,knd->tkgd', rounded, key_value_pair[..., HEAD_SIZE:])
        blended = blended / jnp.transpose(row_total, (2, 0, 1, 3))
        return blended.reshape(TEXT_TOKENS, QUERY_HEADS * HEAD_SIZE).astype(jnp.bfloat16)
    span_outputs = lax.map(span_out, (jnp.arange(SPANS, dtype=jnp.int32), query_heads.reshape(SPANS, TEXT_TOKENS, QUERY_HEADS, HEAD_SIZE), admission))
    return span_outputs.reshape(TEXT, QUERY_HEADS * HEAD_SIZE)
```

```python
import math

import jax
import jax.numpy as jnp
from jax import lax
from jax.experimental import pallas as pl
from jax.experimental.pallas import tpu as pltpu
from jax.sharding import PartitionSpec as P

KEY_VALUE_HEADS = 8
IMAGE_LOOKBACK = 4
PLANE = 4
EPS = 1e-05


def rms_scale(values, gain):
    return values * lax.rsqrt(jnp.mean(values * values, axis=-1, keepdims=True) + EPS) * gain


def swap(value, bit):
    count = lax.axis_size("seq")
    return lax.ppermute(value, "seq", [(i, i ^ bit) for i in range(count)])


def from_plane_before(value):
    count = lax.axis_size("seq")
    return lax.ppermute(value, "seq", [(i, i + PLANE) for i in range(count - PLANE)])


def pack_kernel(*refs):
    *parts, gain, out = refs
    total = parts[0][...].astype(jnp.float32)
    for part in parts[1:]:
        total = total + part[...].astype(jnp.float32)
    head_dim = gain.shape[1]
    out[:, :head_dim] = rms_scale(total[:, :head_dim], gain[...]).astype(out.dtype)
    out[:, head_dim:] = total[:, head_dim:].astype(out.dtype)


def pack(parts, gain):
    tokens, columns = parts[0].shape
    head_dim = gain.shape[1]
    spec = pl.BlockSpec((tokens, 2 * head_dim), lambda h: (0, h))
    return pl.pallas_call(
        pack_kernel,
        grid=(columns // (2 * head_dim),),
        out_shape=jax.ShapeDtypeStruct((tokens, columns), jnp.bfloat16),
        in_specs=[spec] * len(parts) + [pl.BlockSpec((1, head_dim), lambda h: (0, 0))],
        out_specs=spec,
        compiler_params=pltpu.CompilerParams(vmem_limit_bytes=40 << 20),
        cost_estimate=pl.CostEstimate(
            flops=10 * tokens * columns, bytes_accessed=8 * tokens * columns, transcendentals=0
        ),
    )(*parts, gain)


def attend_kernel(n_parts, slots, tile, *refs):
    flags = refs[0]
    parts = refs[1 : 1 + n_parts]
    gain = refs[1 + n_parts]
    images = refs[2 + n_parts : 2 + n_parts + slots]
    out, q_ref, m_ref, l_ref, acc_ref = refs[2 + n_parts + slots :]
    rows = out.shape[0]
    head_dim = gain.shape[1]
    group = out.shape[1] // head_dim
    scale = math.log2(math.e) / math.sqrt(head_dim)
    for j in range(group):
        cols = slice(j * head_dim, (j + 1) * head_dim)
        total = parts[0][:, cols].astype(jnp.float32)
        for part in parts[1:]:
            total = total + part[:, cols].astype(jnp.float32)
        q_ref[j * rows : (j + 1) * rows, :] = rms_scale(total, gain[...]).astype(jnp.bfloat16)

    def one_image(slot):
        image = images[slot]

        @pl.loop(0, group * rows // tile)
        def _(t):
            at = pl.ds(pl.multiple_of(t * tile, tile), tile)
            scores = lax.dot_general(
                q_ref[at, :],
                image[:, :head_dim],
                (((1,), (1,)), ((), ())),
                preferred_element_type=jnp.float32,
            )
            peak = jnp.max(scores, axis=1, keepdims=True)
            if slot > 0:
                before = m_ref[at, :]
                peak = jnp.maximum(peak, before)
            weights = jnp.exp2((scores - peak) * scale)
            total = jnp.sum(weights, axis=1, keepdims=True)
            blended = jnp.dot(
                weights.astype(jnp.bfloat16),
                image[:, head_dim:],
                preferred_element_type=jnp.float32,
            )
            if slot > 0:
                kept = jnp.exp2((before - peak) * scale)
                total = total + kept * l_ref[at, :]
                blended = blended + kept * acc_ref[at, :]
            m_ref[at, :] = peak
            l_ref[at, :] = total
            acc_ref[at, :] = blended

    one_image(0)
    for slot in range(1, slots):
        pl.when(flags[slot] == 1)(lambda slot=slot: one_image(slot))
    for j in range(group):
        at = slice(j * rows, (j + 1) * rows)
        out[:, j * head_dim : (j + 1) * head_dim] = (acc_ref[at, :] / l_ref[at, :]).astype(out.dtype)


def attend(flags, parts, gain, images, first, heads):
    rows = parts[0].shape[0]
    tokens = images[0].shape[0]
    head_dim = gain.shape[1]
    group = parts[0].shape[1] // head_dim // first[1]
    width = group * head_dim
    start = first[0]
    slots = len(images)
    tall = group * rows
    tile = min(512, tall)

    def kernel(*refs):
        attend_kernel(len(parts), slots, tile, *refs)

    return pl.pallas_call(
        kernel,
        grid=(heads,),
        out_shape=jax.ShapeDtypeStruct((rows, heads * width), jnp.bfloat16),
        in_specs=[pl.BlockSpec(memory_space=pltpu.SMEM)]
        + [pl.BlockSpec((rows, width), lambda h: (0, h + start))] * len(parts)
        + [pl.BlockSpec((1, head_dim), lambda h: (0, 0))]
        + [pl.BlockSpec((tokens, 2 * head_dim), lambda h: (0, h))] * slots,
        out_specs=pl.BlockSpec((rows, width), lambda h: (0, h)),
        scratch_shapes=[
            pltpu.VMEM((tall, head_dim), jnp.bfloat16),
            pltpu.VMEM((tall, 1), jnp.float32),
            pltpu.VMEM((tall, 1), jnp.float32),
            pltpu.VMEM((tall, head_dim), jnp.float32),
        ],
        compiler_params=pltpu.CompilerParams(vmem_limit_bytes=48 << 20),
        cost_estimate=pl.CostEstimate(
            flops=12 * heads * tall * tokens * head_dim,
            bytes_accessed=4 * slots * heads * tokens * head_dim,
            transcendentals=3 * heads * tall * tokens,
        ),
    )(flags, *parts, gain, *images)


def on_device(
    text_states,
    images,
    norm_gain,
    query_weight,
    image_projection_weight,
    query_gain,
    key_gain,
    admission,
):
    head_dim = query_gain.shape[0]
    fsdp = lax.axis_size("fsdp")
    seq = lax.axis_size("seq")
    planes = seq // PLANE
    local_kv = KEY_VALUE_HEADS // fsdp
    rows, model = text_states.shape
    depth = query_weight.shape[0]
    index = lax.axis_index("seq")
    mine = lax.axis_index("fsdp")
    place = index % PLANE
    x_place = place // 2
    core = place % 2

    normed = rms_scale(text_states.astype(jnp.float32), norm_gain).astype(jnp.bfloat16)
    by_place = normed.reshape(rows, planes, PLANE, depth)

    def features_of(where):
        part = lax.dynamic_slice_in_dim(by_place, where, 1, 2)
        return part.reshape(rows, planes * depth)

    text_parts = [features_of(place)]
    for bit in range(1, PLANE):
        text_parts.append(swap(features_of(place ^ bit), bit))

    weight_block = lax.all_gather(image_projection_weight, "seq", axis=0, tiled=True)
    query_weight, weight_block = lax.optimization_barrier((query_weight, weight_block))
    groups = [[z * PLANE + p for z in range(planes)] for p in range(PLANE)]
    query_block = lax.all_gather(
        query_weight, "seq", axis=0, tiled=True, axis_index_groups=groups
    )

    features = images[0]
    chunks = 2 if local_kv % 2 == 0 else 1
    heads = local_kv // chunks
    width = heads * 2 * head_dim

    def project(owner, chunk):
        start = owner * (local_kv * 2 * head_dim) + chunk * width
        columns = lax.dynamic_slice_in_dim(weight_block, start, width, 1)
        return jnp.dot(features, columns, preferred_element_type=jnp.float32).astype(jnp.bfloat16)

    def rotate(value, steps):
        return lax.ppermute(value, "fsdp", [(i, (i + steps) % fsdp) for i in range(fsdp)])

    gain_row = key_gain.reshape(1, head_dim)
    sent = [
        [rotate(project((mine + s) % fsdp, c), s) for s in range(1, fsdp)] for c in range(chunks)
    ]
    windows = []
    for c in range(chunks):
        own = pack([project(mine, c)] + sent[c], gain_row)
        before = from_plane_before(own)
        two = swap(jnp.where(x_place == 0, own, before), 2)
        near = swap(jnp.where(core == 0, own, before), 1)
        far = swap(two, 1)
        windows.append([own, before, two, near, far])

    partial = jnp.dot(
        jnp.concatenate(text_parts, axis=0), query_block, preferred_element_type=jnp.float32
    ).astype(jnp.bfloat16)
    query_parts = [partial[:rows]]
    for bit in range(1, PLANE):
        query_parts.append(swap(partial[bit * rows : (bit + 1) * rows], bit))

    near_by = jnp.where(core == 0, 3, 1)
    far_by = jnp.where(core == 0, 1, 3)
    distances = jnp.stack(
        [jnp.int32(0), jnp.int32(PLANE), jnp.int32(2), near_by.astype(jnp.int32), far_by.astype(jnp.int32)]
    )
    image_ids = index - distances
    flags = (image_ids >= 0) & (jnp.take(admission[0], jnp.maximum(image_ids, 0)) == 1)
    flags = flags.astype(jnp.int32)
    outs = [
        attend(
            flags, query_parts, query_gain.reshape(1, head_dim), windows[c], (c * heads, local_kv), heads
        )
        for c in range(chunks)
    ]
    return jnp.concatenate(outs, axis=1) if chunks > 1 else outs[0]


def solution(mesh):
    placed = (
        P("seq", None),
        P("seq", None, "fsdp"),
        P(),
        P("seq", "fsdp"),
        P(("fsdp", "seq"), None),
        P(),
        P(),
        P("seq", None),
    )
    return jax.shard_map(
        on_device, mesh=mesh, in_specs=placed, out_specs=P("seq", "fsdp"), check_vma=False
    )
```

```python
import math

import jax
import jax.numpy as jnp
from jax import lax
from jax.experimental import pallas as pl
from jax.experimental.pallas import tpu as pltpu
from jax.sharding import PartitionSpec as P

KEY_VALUE_HEADS = 8
IMAGE_LOOKBACK = 4
PLANE = 4
EPS = 1e-05


def rms_scale(values, gain):
    return values * lax.rsqrt(jnp.mean(values * values, axis=-1, keepdims=True) + EPS) * gain


def swap(value, bit):
    count = lax.axis_size("seq")
    return lax.ppermute(value, "seq", [(i, i ^ bit) for i in range(count)])


def from_plane_before(value):
    count = lax.axis_size("seq")
    return lax.ppermute(value, "seq", [(i, i + PLANE) for i in range(count - PLANE)])


def pack_kernel(*refs):
    *parts, gain, out = refs
    total = parts[0][...].astype(jnp.float32)
    for part in parts[1:]:
        total = total + part[...].astype(jnp.float32)
    head_dim = gain.shape[1]
    out[:, :head_dim] = rms_scale(total[:, :head_dim], gain[...]).astype(out.dtype)
    out[:, head_dim:] = total[:, head_dim:].astype(out.dtype)


def pack(parts, gain):
    tokens, columns = parts[0].shape
    head_dim = gain.shape[1]
    spec = pl.BlockSpec((tokens, 2 * head_dim), lambda h: (0, h))
    return pl.pallas_call(
        pack_kernel,
        grid=(columns // (2 * head_dim),),
        out_shape=jax.ShapeDtypeStruct((tokens, columns), jnp.bfloat16),
        in_specs=[spec] * len(parts) + [pl.BlockSpec((1, head_dim), lambda h: (0, 0))],
        out_specs=spec,
        compiler_params=pltpu.CompilerParams(vmem_limit_bytes=40 << 20),
        cost_estimate=pl.CostEstimate(
            flops=10 * tokens * columns, bytes_accessed=8 * tokens * columns, transcendentals=0
        ),
    )(*parts, gain)


def attend_kernel(n_parts, slots, tile, *refs):
    flags = refs[0]
    parts = refs[1 : 1 + n_parts]
    gain = refs[1 + n_parts]
    images = refs[2 + n_parts : 2 + n_parts + slots]
    out, q_ref, m_ref, l_ref, acc_ref = refs[2 + n_parts + slots :]
    rows = out.shape[0]
    head_dim = gain.shape[1]
    group = out.shape[1] // head_dim
    scale = math.log2(math.e) / math.sqrt(head_dim)
    for j in range(group):
        cols = slice(j * head_dim, (j + 1) * head_dim)
        total = parts[0][:, cols].astype(jnp.float32)
        for part in parts[1:]:
            total = total + part[:, cols].astype(jnp.float32)
        q_ref[j * rows : (j + 1) * rows, :] = rms_scale(total, gain[...]).astype(jnp.bfloat16)

    def one_image(slot):
        image = images[slot]

        @pl.loop(0, group * rows // tile)
        def _(t):
            at = pl.ds(pl.multiple_of(t * tile, tile), tile)
            scores = lax.dot_general(
                q_ref[at, :],
                image[:, :head_dim],
                (((1,), (1,)), ((), ())),
                preferred_element_type=jnp.float32,
            )
            peak = jnp.max(scores, axis=1, keepdims=True)
            if slot > 0:
                before = m_ref[at, :]
                peak = jnp.maximum(peak, before)
            weights = jnp.exp2((scores - peak) * scale)
            total = jnp.sum(weights, axis=1, keepdims=True)
            blended = jnp.dot(
                weights.astype(jnp.bfloat16),
                image[:, head_dim:],
                preferred_element_type=jnp.float32,
            )
            if slot > 0:
                kept = jnp.exp2((before - peak) * scale)
                total = total + kept * l_ref[at, :]
                blended = blended + kept * acc_ref[at, :]
            m_ref[at, :] = peak
            l_ref[at, :] = total
            acc_ref[at, :] = blended

    one_image(0)
    for slot in range(1, slots):
        pl.when(flags[slot] == 1)(lambda slot=slot: one_image(slot))
    for j in range(group):
        at = slice(j * rows, (j + 1) * rows)
        out[:, j * head_dim : (j + 1) * head_dim] = (acc_ref[at, :] / l_ref[at, :]).astype(out.dtype)


def attend(flags, parts, gain, images, heads):
    rows = parts[0].shape[0]
    tokens = images[0].shape[0]
    head_dim = gain.shape[1]
    group = parts[0].shape[1] // head_dim // heads
    width = group * head_dim
    slots = len(images)
    tall = group * rows
    tile = min(512, tall)

    def kernel(*refs):
        attend_kernel(len(parts), slots, tile, *refs)

    return pl.pallas_call(
        kernel,
        grid=(heads,),
        out_shape=jax.ShapeDtypeStruct((rows, heads * width), jnp.bfloat16),
        in_specs=[pl.BlockSpec(memory_space=pltpu.SMEM)]
        + [pl.BlockSpec((rows, width), lambda h: (0, h))] * len(parts)
        + [pl.BlockSpec((1, head_dim), lambda h: (0, 0))]
        + [pl.BlockSpec((tokens, 2 * head_dim), lambda h: (0, h))] * slots,
        out_specs=pl.BlockSpec((rows, width), lambda h: (0, h)),
        scratch_shapes=[
            pltpu.VMEM((tall, head_dim), jnp.bfloat16),
            pltpu.VMEM((tall, 1), jnp.float32),
            pltpu.VMEM((tall, 1), jnp.float32),
            pltpu.VMEM((tall, head_dim), jnp.float32),
        ],
        compiler_params=pltpu.CompilerParams(vmem_limit_bytes=48 << 20),
        cost_estimate=pl.CostEstimate(
            flops=12 * heads * tall * tokens * head_dim,
            bytes_accessed=4 * slots * heads * tokens * head_dim,
            transcendentals=3 * heads * tall * tokens,
        ),
    )(flags, *parts, gain, *images)


def on_device(
    text_states,
    images,
    norm_gain,
    query_weight,
    image_projection_weight,
    query_gain,
    key_gain,
    admission,
):
    head_dim = query_gain.shape[0]
    fsdp = lax.axis_size("fsdp")
    seq = lax.axis_size("seq")
    planes = seq // PLANE
    local_kv = KEY_VALUE_HEADS // fsdp
    rows, model = text_states.shape
    depth = query_weight.shape[0]
    index = lax.axis_index("seq")
    mine = lax.axis_index("fsdp")
    place = index % PLANE
    x_place = place // 2
    core = place % 2

    normed = rms_scale(text_states.astype(jnp.float32), norm_gain).astype(jnp.bfloat16)
    by_place = normed.reshape(rows, planes, PLANE, depth)

    def features_of(where):
        part = lax.dynamic_slice_in_dim(by_place, where, 1, 2)
        return part.reshape(rows, planes * depth)

    text_sources = [features_of(place ^ bit) for bit in range(PLANE)]

    features = images[0]
    chunks = 2 if local_kv % 2 == 0 else 1
    heads = local_kv // chunks
    width = heads * 2 * head_dim
    query_width = query_weight.shape[1] // chunks
    groups = [[z * PLANE + p for z in range(planes)] for p in range(PLANE)]

    def columns_of(step, chunk):
        start = (mine + step) % fsdp * (local_kv * 2 * head_dim) + chunk * width
        return lax.dynamic_slice_in_dim(image_projection_weight, start, width, 1)

    order = [(s, c) for s in range(1, fsdp) for c in range(chunks)] + [(0, c) for c in range(chunks)]
    query_shards = [
        query_weight[:, c * query_width : (c + 1) * query_width] for c in range(chunks)
    ]
    gathered = []

    def gather(shard, after=(), **options):
        if gathered:
            shard, gathered[-1], after = lax.optimization_barrier((shard, gathered[-1], after))
        gathered.append(lax.all_gather(shard, "seq", axis=0, tiled=True, **options))
        return after

    def project(step):
        product = jnp.dot(features, gathered[step], preferred_element_type=jnp.float32)
        return product.astype(jnp.bfloat16)

    def rotate(value, steps):
        return lax.ppermute(value, "fsdp", [(i, (i + steps) % fsdp) for i in range(fsdp)])

    gain_row = key_gain.reshape(1, head_dim)
    sent = {}
    windows = []
    text = None
    gather(columns_of(*order[0]))
    for step, key in enumerate(order):
        later = order[step + 1] if step + 1 < len(order) else None
        if step == 0:
            text_sources = gather(columns_of(*later), text_sources)
            text_parts = text_sources[:1]
            for bit in range(1, PLANE):
                text_parts.append(swap(text_sources[bit], bit))
        else:
            if step == 1:
                after = text_parts
            else:
                after = [sent[order[step - 2]]] if order[step - 2] in sent else []
            if later is not None:
                after = gather(columns_of(*later), after)
            else:
                after = gather(query_shards[0], after, axis_index_groups=groups)
            if step == 1:
                text = jnp.concatenate(after, axis=0)
            elif after:
                sent[order[step - 2]] = after[0]
        if key[0] > 0:
            sent[key] = rotate(project(step), key[0])
        else:
            own = pack([project(step)] + [sent[s, key[1]] for s in range(1, fsdp)], gain_row)
            before = from_plane_before(own)
            windows.append([own, before])

    def relay(own, before):
        two = swap(jnp.where(x_place == 0, own, before), 2)
        near = swap(jnp.where(core == 0, own, before), 1)
        return [own, before, two, near]

    windows[0] = relay(*windows[0])
    for shard in query_shards[1:]:
        windows[0][2], windows[1][1] = gather(
            shard, [windows[0][2], windows[1][1]], axis_index_groups=groups
        )
    windows[1:] = [relay(*window) for window in windows[1:]]
    for window in windows:
        window.append(swap(window[2], 1))
    query_blocks = gathered[len(order) :]

    query_parts = []
    for c in range(chunks):
        partial = jnp.dot(text, query_blocks[c], preferred_element_type=jnp.float32)
        partial = partial.astype(jnp.bfloat16)
        parts = [partial[:rows]]
        for bit in range(1, PLANE):
            parts.append(swap(partial[bit * rows : (bit + 1) * rows], bit))
        query_parts.append(parts)

    near_by = jnp.where(core == 0, 3, 1)
    far_by = jnp.where(core == 0, 1, 3)
    distances = jnp.stack(
        [jnp.int32(0), jnp.int32(PLANE), jnp.int32(2), near_by.astype(jnp.int32), far_by.astype(jnp.int32)]
    )
    image_ids = index - distances
    flags = (image_ids >= 0) & (jnp.take(admission[0], jnp.maximum(image_ids, 0)) == 1)
    flags = flags.astype(jnp.int32)
    outs = [
        attend(
            flags, query_parts[c], query_gain.reshape(1, head_dim), windows[c], heads
        )
        for c in range(chunks)
    ]
    return jnp.concatenate(outs, axis=1) if chunks > 1 else outs[0]


def solution(mesh):
    placed = (
        P("seq", None),
        P("seq", None, "fsdp"),
        P(),
        P("seq", "fsdp"),
        P(("fsdp", "seq"), None),
        P(),
        P(),
        P("seq", None),
    )
    return jax.shard_map(
        on_device, mesh=mesh, in_specs=placed, out_specs=P("seq", "fsdp"), check_vma=False
    )
```
